512 devices in a mesh: blk: 8 (over z_lo, core), grp: 64 (over x, y, z_hi).
Axes of the slice: x: 4, y: 4, z: 16 (z_hi: 4, z_lo: 4; z = z_hi * 4 + z_lo), core: 2. Of those that a mesh axis runs over, the one named last changes fastest.
Arguments:
- images: bfloat16 [131072, 1152], P(('blk', 'grp')), may hold values from -0.19921875 to 0.19921875
- texts: bfloat16 [1024, 1152], P(('blk', 'grp')), may hold values from -6 to 6
- text_proj: bfloat16 [1152, 1152], replicated, may hold values from -0.1875 to 0.1875
- labels: int32 [131072], P(('blk', 'grp')), may hold values from 0 to 1023
- logit_scale: float32 [1], replicated, may hold values from 4 to 16
- logit_bias: float32 [1], replicated, may hold values from -4 to -2
Outputs:
- image_grads: bfloat16 [131072, 1152], P(('blk', 'grp'))
- text_grads: float32 [1024, 1152], P(('blk', 'grp'))
The draws below stay inside these ranges and needn't reach their ends.
All inputs are finite; a program needn't handle non-finite values.
Results may differ from the reference program's by a relative error of at most 0.012.
Values may be sent and summed in bfloat16 or wider, within the bound.
A program may use at most 64 MiB of HBM per device.

```python
import math
import jax
import jax.numpy as jnp
from jax import lax

D = 1152
IMAGES = 131072
TEXTS = 1024


def place_ends(drawn, own_key, least, top_value):
    longest = drawn.shape.index(max(drawn.shape))
    spots = []
    for shift in (0, 1):
        where = [jax.random.randint(jax.random.fold_in(own_key, axis), (), 0, length) for axis, length in enumerate(drawn.shape)]
        where[longest] = (where[longest] + shift) % drawn.shape[longest]
        spots.append(tuple(where))
    return drawn.at[spots[0]].set(least).at[spots[1]].set(top_value)


def shard_levels(stream_key, dims, split, low, top_value):
    level = 1.0
    for position, shards_of in split:
        steps = jax.random.uniform(jax.random.fold_in(jax.random.fold_in(stream_key, 6), position), (shards_of,), jnp.float32, low / len(split), top_value / len(split))
        level = level * jnp.repeat(jnp.exp(steps), dims[position] // shards_of).reshape((-1,) + (1,) * (len(dims) - 1 - position))
    return level


def scatter_about(own_key, extent, deviation, most, split=(), held_as=jnp.bfloat16):
    result = deviation * jax.random.normal(own_key, extent, jnp.float32)
    if split:
        result = result * shard_levels(own_key, extent, split, -0.22, 0.18)
    return jnp.clip(result, -most, most).astype(held_as)


def setup_inputs(seed: int = 0) -> dict:
    splits = jax.random.split(jax.random.key(seed), 7)
    return {
        "images": scatter_about(splits[0], (IMAGES, D), 0.03, 0.19921875, ((0, 512),)),
        "texts": scatter_about(splits[1], (TEXTS, D), 1.0, 6.0, ((0, 512),)),
        "text_proj": scatter_about(splits[2], (D, D), D ** -0.5, 0.1875),
        "labels": place_ends(jax.random.randint(splits[3], (IMAGES,), 0, TEXTS), jax.random.fold_in(splits[3], 1), 0, TEXTS - 1).astype(jnp.int32),
        "logit_scale": jnp.clip(jnp.exp(jax.random.uniform(splits[4], (1,), jnp.float32, math.log(4.0), math.log(16.0))), 4.0, 16.0),
        "logit_bias": jnp.clip(jax.random.uniform(splits[5], (1,), jnp.float32, -4.0, -2.0), -4.0, -2.0),
    }


def reference(images, texts, text_proj, labels, logit_scale, logit_bias):
    feats = images.astype(jnp.float32)
    rinv_x = lax.rsqrt(lax.optimization_barrier(jnp.sum(feats * feats, axis=-1, keepdims=True)) + 1e-06)
    unit_img = feats * rinv_x
    img_emb = unit_img.astype(jnp.bfloat16)
    proj = jnp.dot(texts, text_proj, preferred_element_type=jnp.float32)
    rinv_y = lax.rsqrt(lax.optimization_barrier(jnp.sum(proj * proj, axis=-1, keepdims=True)) + 1e-06)
    unit_txt = proj * rinv_y
    txt_emb = unit_txt.astype(jnp.bfloat16)
    scale = logit_scale[0]
    bias = logit_bias[0]
    columns = jnp.arange(TEXTS, dtype=jnp.int32)
    rows = math.gcd(IMAGES, 4096)
    emb_blocks = img_emb.reshape(IMAGES // rows, rows, D)
    label_blocks = labels.reshape(IMAGES // rows, rows)

    def one_block(carry, inputs):
        emb, lab = inputs
        logits = scale * jnp.dot(emb, txt_emb.T, preferred_element_type=jnp.float32) + bias
        sign = jnp.where(lab[:, None] == columns[None, :], 1.0, -1.0).astype(logits.dtype)
        dlogit = -sign * jax.nn.sigmoid(-sign * logits)
        weighted = (scale * dlogit).astype(jnp.bfloat16)
        grad_img = jnp.dot(weighted, txt_emb, preferred_element_type=jnp.float32)
        carry = carry + jnp.dot(weighted.T, emb, preferred_element_type=jnp.float32)
        return (carry, grad_img)
    start = jnp.zeros((TEXTS, D), jnp.float32)
    emb_grad_txt, grad_blocks = lax.scan(one_block, start, (emb_blocks, label_blocks))
    emb_grad_img = grad_blocks.reshape(IMAGES, D)
    image_grads = ((emb_grad_img - unit_img * lax.optimization_barrier(jnp.sum(unit_img * emb_grad_img, axis=-1, keepdims=True))) * rinv_x).astype(jnp.bfloat16)
    proj_grad = ((emb_grad_txt - unit_txt * lax.optimization_barrier(jnp.sum(unit_txt * emb_grad_txt, axis=-1, keepdims=True))) * rinv_y).astype(jnp.bfloat16)
    text_grads = jnp.dot(proj_grad, text_proj.T, preferred_element_type=jnp.float32)
    return (image_grads, text_grads)
```

```python
import functools

import jax
import jax.numpy as jnp
from jax import lax
from jax.experimental import pallas as pl
from jax.experimental.pallas import tpu as pltpu
from jax.sharding import PartitionSpec as P

MESH = pl.DeviceIdType.MESH
BF = jnp.bfloat16
F32 = jnp.float32
D = 1152
NI = 256
EPS = 1e-06
NT = (((1,), (1,)), ((), ()))
TN = (((0,), (0,)), ((), ()))


def mod(a, n):
    return lax.rem(a + n, n)


def device(x, y, z, c):
    return {
        "blk": lax.rem(z, 4) * 2 + c,
        "grp": x * 16 + y * 4 + lax.div(z, 4),
    }


def sigmoid_grad(logits, match, scale):
    t = jnp.where(match, -logits, logits)
    s = scale / (1.0 + jnp.exp(-t))
    return jnp.where(match, -s, s).astype(BF)


def kernel(
    images, texts, proj_w, labels, scale_ref, bias_ref,
    out_img, out_txt,
    imgs, emb, wv, lab2, zin, ta, tb, e_txt, wt, proj_own, gtx, gimg_out, gimg_in, outv,
    s1a, s1b, r1a, r1b, acc_a, acc_b, s2a, s2b, r2a, r2b, fa, fb, zout, zr,
    sem_local, sem_core_s, sem_core_r, sem_z_s, sem_z_r, sem_s_s, sem_s_r,
    sem_b_s, sem_b_r, sem_r1_s, sem_r1_r, sem_r2_s, sem_r2_r, sem_r3_s, sem_r3_r,
):
    blk = lax.axis_index("blk")
    grp = lax.axis_index("grp")
    c = lax.rem(blk, 2)
    z = lax.rem(grp, 4) * 4 + lax.div(blk, 2)
    x = lax.div(grp, 16)
    y = lax.rem(lax.div(grp, 4), 4)

    def remote(src, dst, ss, rs, dx=0, dy=0, dz=0, dc=0):
        return pltpu.make_async_remote_copy(
            src_ref=src, dst_ref=dst, send_sem=ss, recv_sem=rs,
            device_id=device(mod(x + dx, 4), mod(y + dy, 4), mod(z + dz, 16), mod(c + dc, 2)),
            device_id_type=MESH,
        )

    load_img = pltpu.make_async_copy(images, imgs.at[0], sem_local.at[0])
    load_w = pltpu.make_async_copy(proj_w, wv, sem_local.at[1])
    load_img.start()
    load_w.start()

    barrier = pltpu.get_barrier_semaphore()
    partners = [dict(dc=1)] + [dict(dx=d) for d in (1, 2, 3)] + [dict(dy=d) for d in (1, 2, 3)]
    partners += [dict(dz=d) for d in range(1, 16)]
    for p in partners:
        who = device(mod(x + p.get("dx", 0), 4), mod(y + p.get("dy", 0), 4),
                     mod(z + p.get("dz", 0), 16), mod(c + p.get("dc", 0), 2))
        pl.semaphore_signal(barrier, inc=1, device_id=who, device_id_type=MESH)
    pl.semaphore_wait(barrier, len(partners))

    zs = [remote(texts, zin.at[z], sem_z_s.at[d], sem_z_r.at[d], dz=d) for d in range(1, 16)]
    for cp in zs:
        cp.start()
    core_img = remote(images, imgs.at[1], sem_core_s.at[0], sem_core_r.at[0], dc=1)
    core_lab = remote(labels, lab2.at[1], sem_core_s.at[1], sem_core_r.at[1], dc=1)
    core_lab.start()
    core_img.start()
    zin[z] = texts[...]
    lab2[0] = labels[...]

    load_w.wait()
    proj_own[...] = jnp.dot(texts[...], wv[...], preferred_element_type=F32)

    def embed(half):
        def step(i, carry):
            rows = pl.ds(pl.multiple_of(i * 64, 64), 64)
            f = imgs[half, rows, :].astype(F32)
            r = lax.rsqrt(jnp.sum(f * f, axis=-1, keepdims=True) + EPS)
            emb[pl.ds(pl.multiple_of(half * NI + i * 64, 64), 64), :] = (f * r).astype(BF)
            return carry
        lax.fori_loop(0, NI // 64, step, 0)

    load_img.wait()
    embed(0)
    core_img.wait()
    core_lab.wait()
    embed(1)

    for cp in zs:
        cp.wait()
    zall = zin[...].astype(F32)
    ta[y, x] = zall[:, 0, :].astype(BF)
    tb[x, y] = zall[:, 1, :].astype(BF)

    small_a = [remote(ta.at[y, x], ta.at[y, x], sem_s_s.at[0, d], sem_s_r.at[0, d], dx=d) for d in (1, 2, 3)]
    small_b = [remote(tb.at[x, y], tb.at[x, y], sem_s_s.at[1, d], sem_s_r.at[1, d], dy=d) for d in (1, 2, 3)]
    for a, b in zip(small_a, small_b):
        a.start()
        b.start()
    bulk = []

    def forward(e):
        xs, ys = mod(x - e, 4), mod(y - e, 4)
        for d in (1, 3, 2):
            a = remote(ta.at[y, xs], ta.at[y, xs], sem_b_s.at[0, e, d], sem_b_r.at[0, e, d], dy=d)
            b = remote(tb.at[x, ys], tb.at[x, ys], sem_b_s.at[1, e, d], sem_b_r.at[1, e, d], dx=d)
            a.start()
            b.start()
            bulk.append(a)
            bulk.append(b)

    forward(0)
    for e in (1, 3, 2):
        small_a[e - 1].wait_recv()
        small_b[e - 1].wait_recv()
        forward(e)
    for cp in small_a + small_b:
        cp.wait_send()
    for cp in bulk:
        cp.wait()

    def project(i, carry):
        h = lax.div(i, 2)
        for part, t in ((0, ta), (1, tb)):
            @pl.when(h == part)
            def _():
                k = lax.rem(i, 2) * 2
                rows = t[pl.ds(k, 2)].reshape(128, D)
                p = jnp.dot(rows, wv[...], preferred_element_type=F32)
                r = lax.rsqrt(jnp.sum(p * p, axis=-1, keepdims=True) + EPS)
                e_txt[pl.ds(pl.multiple_of(i * 128, 128), 128), :] = (p * r).astype(BF)
        return carry

    lax.fori_loop(0, 4, project, 0)

    scale = scale_ref[0]
    bias = bias_ref[0]

    lab = jnp.concatenate([lab2[0][None, :], lab2[1][None, :]], axis=1)
    lr = lab & 1
    lz = ((lab >> 1) & 3) * 4 + ((lab >> 8) & 3)
    ly = (lab >> 3) & 3
    lx = (lab >> 5) & 3
    lc = (lab >> 7) & 1
    pos = jnp.where(lr == 0, (ly * 4 + lx) * 16 + lz, 256 + (lx * 4 + ly) * 16 + lz)
    pos = jnp.where(lc == c, pos, -1)

    def weigh(i, carry):
        rows = pl.ds(pl.multiple_of(i * 128, 128), 128)
        logits = lax.dot_general(e_txt[rows, :], emb[...], NT, preferred_element_type=F32)
        logits = scale * logits + bias
        ids = lax.broadcasted_iota(jnp.int32, logits.shape, 0) + i * 128
        w = sigmoid_grad(logits, ids == pos, scale)
        wt[rows, :] = w
        g = jnp.dot(w, emb[...], preferred_element_type=F32)
        gtx[rows, :] = g
        return carry

    lax.fori_loop(0, 4, weigh, 0)

    r1 = []
    for d in (2, 1, 3):
        yy, xx = mod(y + d, 4), mod(x + d, 4)
        s1a[d - 1] = gtx[pl.ds(pl.multiple_of(yy * 64, 64), 64), :].astype(BF)
        s1b[d - 1] = gtx[pl.ds(pl.multiple_of(256 + xx * 64, 64), 64), :].astype(BF)
        a = remote(s1a.at[d - 1], r1a.at[d - 1], sem_r1_s.at[0, d], sem_r1_r.at[0, d], dy=d)
        b = remote(s1b.at[d - 1], r1b.at[d - 1], sem_r1_s.at[1, d], sem_r1_r.at[1, d], dx=d)
        a.start()
        b.start()
        r1 += [a, b]

    def image_part(half):
        def step(i, carry):
            cols = pl.ds(pl.multiple_of(half * NI + i * 128, 128), 128)
            g = lax.dot_general(wt[:, cols], e_txt[...], TN, preferred_element_type=F32)
            rows = pl.ds(pl.multiple_of(i * 128, 128), 128)
            if half == 1:
                gimg_out[rows, :] = g.astype(BF)
            else:
                outv[rows, :] = g
            return carry
        lax.fori_loop(0, 2, step, 0)

    image_part(1)
    core_grad = remote(gimg_out, gimg_in, sem_core_s.at[2], sem_core_r.at[2], dc=1)
    core_grad.start()
    image_part(0)

    for cp in r1:
        cp.wait()
    own = gtx[pl.ds(pl.multiple_of(y * 64, 64), 64), :]
    acc_a[...] = own + r1a[0].astype(F32) + r1a[1].astype(F32) + r1a[2].astype(F32)
    own = gtx[pl.ds(pl.multiple_of(256 + x * 64, 64), 64), :]
    acc_b[...] = own + r1b[0].astype(F32) + r1b[1].astype(F32) + r1b[2].astype(F32)
    r2 = []
    for d in (2, 1, 3):
        xx, yy = mod(x + d, 4), mod(y + d, 4)
        s2a[d - 1] = acc_a[pl.ds(pl.multiple_of(xx * 16, 16), 16), :].astype(BF)
        s2b[d - 1] = acc_b[pl.ds(pl.multiple_of(yy * 16, 16), 16), :].astype(BF)
        a = remote(s2a.at[d - 1], r2a.at[d - 1], sem_r2_s.at[0, d], sem_r2_r.at[0, d], dx=d)
        b = remote(s2b.at[d - 1], r2b.at[d - 1], sem_r2_s.at[1, d], sem_r2_r.at[1, d], dy=d)
        a.start()
        b.start()
        r2 += [a, b]
    for cp in r2:
        cp.wait()
    own = acc_a[pl.ds(pl.multiple_of(x * 16, 16), 16), :]
    sum_a = own + r2a[0].astype(F32) + r2a[1].astype(F32) + r2a[2].astype(F32)
    own = acc_b[pl.ds(pl.multiple_of(y * 16, 16), 16), :]
    sum_b = own + r2b[0].astype(F32) + r2b[1].astype(F32) + r2b[2].astype(F32)
    fa[...] = sum_a
    fb[...] = sum_b
    for k in range(16):
        zout[k] = jnp.concatenate([sum_a[k : k + 1, :], sum_b[k : k + 1, :]], axis=0).astype(BF)
    r3 = []
    for d in (8, 7, 9, 6, 10, 5, 11, 4, 12, 3, 13, 2, 14, 1, 15):
        cp = remote(zout.at[mod(z + d, 16)], zr.at[d], sem_r3_s.at[d], sem_r3_r.at[d], dz=d)
        cp.start()
        r3.append(cp)

    core_grad.wait()

    def finish(i, carry):
        rows = pl.ds(pl.multiple_of(i * 64, 64), 64)
        g = outv[rows, :] + gimg_in[rows, :].astype(F32)
        f = imgs[0, rows, :].astype(F32)
        r = lax.rsqrt(jnp.sum(f * f, axis=-1, keepdims=True) + EPS)
        u = f * r
        g = (g - u * jnp.sum(u * g, axis=-1, keepdims=True)) * r
        gimg_out[rows, :] = g.astype(BF)
        return carry

    lax.fori_loop(0, NI // 64, finish, 0)
    store = pltpu.make_async_copy(gimg_out, out_img, sem_local.at[2])
    store.start()

    for cp in r3:
        cp.wait()
    total = jnp.concatenate([fa[pl.ds(z, 1), :], fb[pl.ds(z, 1), :]], axis=0)
    for d in range(1, 16):
        total = total + zr[d].astype(F32)
    p = proj_own[...]
    r = lax.rsqrt(jnp.sum(p * p, axis=-1, keepdims=True) + EPS)
    u = p * r
    pg = ((total - u * jnp.sum(u * total, axis=-1, keepdims=True)) * r).astype(BF)
    out_txt[...] = lax.dot_general(pg, wv[...], NT, preferred_element_type=F32)
    store.wait()


def local(images, texts, text_proj, labels, logit_scale, logit_bias):
    vmem = pl.BlockSpec(memory_space=pltpu.VMEM)
    smem = pl.BlockSpec(memory_space=pltpu.SMEM)
    hbm = pl.BlockSpec(memory_space=pl.ANY)
    dma = pltpu.SemaphoreType.DMA
    scratch = [
        pltpu.VMEM((2, NI, D), BF),
        pltpu.VMEM((2 * NI, D), BF),
        pltpu.VMEM((D, D), BF),
        pltpu.VMEM((2, NI), jnp.int32),
        pltpu.VMEM((16, 2, D), BF),
        pltpu.VMEM((4, 4, 16, D), BF),
        pltpu.VMEM((4, 4, 16, D), BF),
        pltpu.VMEM((512, D), BF),
        pltpu.VMEM((512, 2 * NI), BF),
        pltpu.VMEM((2, D), F32),
        pltpu.VMEM((512, D), F32),
        pltpu.VMEM((NI, D), BF),
        pltpu.VMEM((NI, D), BF),
        pltpu.VMEM((NI, D), F32),
        pltpu.VMEM((3, 64, D), BF),
        pltpu.VMEM((3, 64, D), BF),
        pltpu.VMEM((3, 64, D), BF),
        pltpu.VMEM((3, 64, D), BF),
        pltpu.VMEM((64, D), F32),
        pltpu.VMEM((64, D), F32),
        pltpu.VMEM((3, 16, D), BF),
        pltpu.VMEM((3, 16, D), BF),
        pltpu.VMEM((3, 16, D), BF),
        pltpu.VMEM((3, 16, D), BF),
        pltpu.VMEM((16, D), F32),
        pltpu.VMEM((16, D), F32),
        pltpu.VMEM((16, 2, D), BF),
        pltpu.VMEM((16, 2, D), BF),
        dma((3,)), dma((3,)), dma((3,)), dma((16,)), dma((16,)), dma((2, 4)), dma((2, 4)),
        dma((2, 4, 4)), dma((2, 4, 4)), dma((2, 4)), dma((2, 4)), dma((2, 4)), dma((2, 4)),
        dma((16,)), dma((16,)),
    ]
    return pl.pallas_call(
        kernel,
        out_shape=(
            jax.ShapeDtypeStruct((NI, D), BF),
            jax.ShapeDtypeStruct((2, D), F32),
        ),
        in_specs=[hbm, vmem, hbm, vmem, smem, smem],
        out_specs=(hbm, vmem),
        scratch_shapes=scratch,
        compiler_params=pltpu.CompilerParams(
            collective_id=0, has_side_effects=True, vmem_limit_bytes=50 * 2**20
        ),
        cost_estimate=pl.CostEstimate(flops=4 * 10**9, bytes_accessed=8 * 10**6, transcendentals=10**6),
        name="reward_backward",
    )(images, texts, text_proj, labels, logit_scale, logit_bias)


def solution(mesh):
    in_specs = (P(("blk", "grp"), None), P(("blk", "grp"), None), P(), P(("blk", "grp")), P(), P())
    out_specs = (P(("blk", "grp"), None), P(("blk", "grp"), None))
    return jax.shard_map(local, mesh=mesh, in_specs=in_specs, out_specs=out_specs, check_vma=False)
```

```python
import jax
import jax.numpy as jnp
from jax import lax
from jax.experimental import pallas as pl
from jax.experimental.pallas import tpu as pltpu
from jax.sharding import PartitionSpec as P

MESH = pl.DeviceIdType.MESH
BF = jnp.bfloat16
F32 = jnp.float32
D = 1152
NI = 256
EPS = 1e-06
NT = (((1,), (1,)), ((), ()))
TN = (((0,), (0,)), ((), ()))
STEPS = (0, -1, -2, -3, 1, 2, 3, 4, 5, 6, 7, 8, -4, -5, -6, -7)
NEAR = (7, 6, 3, 5, 2, 4, 1)
SEG = 128


def mod(a, n):
    return lax.rem(a + n, n)


def unit(v):
    r = lax.rsqrt(jnp.sum(v * v, axis=-1, keepdims=True) + EPS)
    return v * r, r


def kernel(
    images, texts, proj_w, labels, scale_ref, bias_ref,
    out_img, out_txt,
    scal, imgs, emb, wv, lab_a, lab_b, zin, tx, e_txt, wt, proj_own, gimg_out, gimg_in, gimg,
    own1, s1, r1, own2, s2, r2, own3, zout, zr,
    sem_l, sem_cs, sem_cr, sem_zs, sem_zr, sem_ss, sem_sr, sem_bs, sem_br,
    sem_1s, sem_1r, sem_2s, sem_2r, sem_3s, sem_3r,
):
    blk = lax.axis_index("blk")
    grp = lax.axis_index("grp")
    c = lax.rem(blk, 2)
    z = lax.rem(grp, 4) * 4 + lax.div(blk, 2)
    x = lax.div(grp, 16)
    y = lax.rem(lax.div(grp, 4), 4)

    def device(dx=0, dy=0, dz=0, dc=0):
        tz = mod(z + dz, 16)
        return {
            "blk": lax.rem(tz, 4) * 2 + mod(c + dc, 2),
            "grp": mod(x + dx, 4) * 16 + mod(y + dy, 4) * 4 + lax.div(tz, 4),
        }

    def remote(src, dst, ss, rs, **to):
        return pltpu.make_async_remote_copy(
            src_ref=src, dst_ref=dst, send_sem=ss, recv_sem=rs,
            device_id=device(**to), device_id_type=MESH,
        )

    def along(half, by, first):
        return {"dx" if (half == 0) == first else "dy": by}

    loads = [
        pltpu.make_async_copy(texts, zin.at[0], sem_l.at[0]),
        pltpu.make_async_copy(labels, lab_a, sem_l.at[1]),
        pltpu.make_async_copy(images, imgs.at[0], sem_l.at[2]),
        pltpu.make_async_copy(proj_w, wv, sem_l.at[3]),
        pltpu.make_async_copy(scale_ref, scal.at[0], sem_l.at[5]),
        pltpu.make_async_copy(bias_ref, scal.at[1], sem_l.at[6]),
    ]
    for cp in loads:
        cp.start()

    barrier = pltpu.get_barrier_semaphore()
    partners = [dict(dz=d) for d in (4, -4, 3, -3, 2, -2, 1, -1)]
    partners += [dict(dx=d) for d in (1, 2, 3)] + [dict(dy=d) for d in (1, 2, 3)] + [dict(dc=1)]
    for p in partners:
        pl.semaphore_signal(barrier, inc=1, device_id=device(**p), device_id_type=MESH)
    for cp in loads:
        cp.wait()
    pl.semaphore_wait(barrier, len(partners))

    zs = {}
    for k in NEAR:
        zs[k] = remote(zin.at[0], zin.at[k], sem_zs.at[k], sem_zr.at[k], dz=STEPS[k])
        zs[k].start()
    core_lab = remote(lab_a, lab_b, sem_cs.at[0], sem_cr.at[0], dc=1)
    core_img = remote(imgs.at[0], imgs.at[1], sem_cs.at[1], sem_cr.at[1], dc=1)
    core_lab.start()
    core_img.start()

    proj_own[...] = jnp.dot(zin[0], wv[...], preferred_element_type=F32)

    def embed(half):
        def step(i, carry):
            u, _ = unit(imgs[half, pl.ds(pl.multiple_of(i * 64, 64), 64), :].astype(F32))
            emb[pl.ds(pl.multiple_of(half * NI + i * 64, 64), 64), :] = u.astype(BF)
            return carry
        lax.fori_loop(0, NI // 64, step, 0)

    embed(0)

    def small(s):
        copies = []
        for d in (2, 1, 3):
            cp = remote(tx.at[s, 0, 0], tx.at[s, 0, d], sem_ss.at[s, d], sem_sr.at[s, d], **along(s % 2, d, True))
            cp.start()
            copies.append(cp)
        return copies

    def spread(s, arriving):
        for cp in arriving:
            cp.wait_recv()
        copies = []
        for d in (2, 1, 3):
            cp = remote(tx.at[s, 0], tx.at[s, d], sem_bs.at[s, d], sem_br.at[s, d], **along(s % 2, d, False))
            cp.start()
            copies.append(cp)
        return copies

    def place(s):
        for k in range(4 * s, 4 * s + 4):
            if k:
                zs[k].wait_recv()
        tx[s, 0, 0] = zin[4 * s : 4 * s + 4].astype(F32).reshape(8, D).astype(BF)
        on = remote(tx.at[s, 0, 0], tx.at[3 - s, 0, 0], sem_zs.at[8 + s], sem_zr.at[8 + s], dz=(-4, 4)[s])
        on.start()
        return on

    on0 = place(0)
    small0 = small(0)
    on1 = place(1)
    small1 = small(1)
    bulk0 = spread(0, small0)
    bulk1 = spread(1, small1)
    core_lab.wait()
    core_img.wait()
    embed(1)
    on0.wait_recv()
    small3 = small(3)
    on1.wait_recv()
    small2 = small(2)
    bulk3 = spread(3, small3)
    bulk2 = spread(2, small2)

    scale = scal[0, 0, 0]
    bias = scal[1, 0, 0]

    lab = jnp.concatenate([lab_a[...][None, :], lab_b[...][None, :]], axis=1)
    ez = mod(z - (((lab >> 1) & 3) * 4 + ((lab >> 8) & 3)), 16)
    ey = mod(y - ((lab >> 3) & 3), 4)
    ex = mod(x - ((lab >> 5) & 3), 4)
    kz = jnp.where(ez == 0, 0, jnp.where(ez <= 8, ez + 3, jnp.where(ez >= 13, 16 - ez, 24 - ez)))
    seg = kz >> 2
    first_axis = (seg & 1) == 0
    i2 = jnp.where(first_axis, ey, ex)
    i1 = jnp.where(first_axis, ex, ey)
    pos = seg * SEG + i2 * 32 + i1 * 8 + (kz & 3) * 2 + (lab & 1)
    pos = jnp.where(((lab >> 7) & 1) == c, pos, -1)

    def segment(s, copies):
        half = s % 2
        for cp in copies:
            cp.wait_recv()
        rows = pl.ds(s * SEG, SEG)
        p = jnp.dot(tx[s].reshape(SEG, D), wv[...], preferred_element_type=F32)
        e = unit(p)[0].astype(BF)
        e_txt[rows, :] = e
        logits = scale * lax.dot_general(e, emb[...], NT, preferred_element_type=F32) + bias
        match = lax.broadcasted_iota(jnp.int32, logits.shape, 0) + s * SEG == pos
        sg = scale / (1.0 + jnp.exp(jnp.where(match, logits, -logits)))
        w = jnp.where(match, -sg, sg).astype(BF)
        wt[rows, :] = w
        g = jnp.dot(w, emb[...], preferred_element_type=F32)
        own1[s] = g[:32]
        s1[s] = g.astype(BF).reshape(4, 32, D)
        sends = []
        for d in (2, 1, 3):
            cp = remote(s1.at[s, d], r1.at[s, d], sem_1s.at[s, d], sem_1r.at[s, d], **along(half, -d, False))
            cp.start()
            sends.append(cp)
        return sends

    first = {0: segment(0, bulk0), 1: segment(1, bulk1)}
    first[3] = segment(3, bulk3)
    first[2] = segment(2, bulk2)

    def image_part(half):
        def step(i, carry):
            cols = pl.ds(pl.multiple_of(half * NI + i * 128, 128), 128)
            g = lax.dot_general(wt[:, cols], e_txt[...], TN, preferred_element_type=F32)
            rows = pl.ds(pl.multiple_of(i * 128, 128), 128)
            if half == 1:
                gimg_out[rows, :] = g.astype(BF)
            else:
                gimg[rows, :] = g
            return carry
        lax.fori_loop(0, 2, step, 0)

    image_part(1)
    core_grad = remote(gimg_out, gimg_in, sem_cs.at[2], sem_cr.at[2], dc=1)
    core_grad.start()

    def second(s):
        half = s % 2
        for cp in first[s]:
            cp.wait_recv()
        acc = own1[s] + r1[s, 1].astype(F32) + r1[s, 2].astype(F32) + r1[s, 3].astype(F32)
        own2[s] = acc[:8]
        s2[s] = acc.astype(BF).reshape(4, 8, D)
        sends = []
        for d in (2, 1, 3):
            cp = remote(s2.at[s, d], r2.at[s, d], sem_2s.at[s, d], sem_2r.at[s, d], **along(half, -d, True))
            cp.start()
            sends.append(cp)
        return sends

    def third(s, sends):
        for cp in sends:
            cp.wait_recv()
        acc = own2[s] + r2[s, 1].astype(F32) + r2[s, 2].astype(F32) + r2[s, 3].astype(F32)
        out = []
        for i in (3, 2, 1, 0):
            k = 4 * s + i
            row = acc[2 * i : 2 * i + 2, :]
            if k == 0:
                own3[...] = row
            else:
                zout[k] = row.astype(BF)
                cp = remote(zout.at[k], zr.at[k], sem_3s.at[k], sem_3r.at[k], dz=-STEPS[k])
                cp.start()
                out.append(cp)
        return out

    second0, second1 = second(0), second(1)
    image_part(0)
    second3, second2 = second(3), second(2)
    seconds = second0 + second1 + second2 + second3
    thirds = third(0, second0) + third(1, second1)
    thirds += third(3, second3) + third(2, second2)

    core_grad.wait()

    def finish(i, carry):
        rows = pl.ds(pl.multiple_of(i * 64, 64), 64)
        g = gimg[rows, :] + gimg_in[rows, :].astype(F32)
        u, r = unit(imgs[0, rows, :].astype(F32))
        g = (g - u * jnp.sum(u * g, axis=-1, keepdims=True)) * r
        gimg_out[rows, :] = g.astype(BF)
        return carry

    lax.fori_loop(0, NI // 64, finish, 0)
    store = pltpu.make_async_copy(gimg_out, out_img, sem_l.at[4])
    store.start()

    sent = list(zs.values()) + [on0, on1] + small0 + small1 + small2 + small3 + bulk0 + bulk1 + bulk2 + bulk3
    sent += first[0] + first[1] + first[2] + first[3] + seconds + thirds
    for cp in sent:
        cp.wait_send()
    store.wait()
    u, r = unit(proj_own[...])

    for cp in thirds:
        cp.wait_recv()
    total = own3[...]
    for k in range(1, 16):
        total = total + zr[k].astype(F32)
    pg = ((total - u * jnp.sum(u * total, axis=-1, keepdims=True)) * r).astype(BF)
    out_txt[...] = lax.dot_general(pg, wv[...], NT, preferred_element_type=F32)


def local(images, texts, text_proj, labels, logit_scale, logit_bias):
    vmem = pl.BlockSpec(memory_space=pltpu.VMEM)
    hbm = pl.BlockSpec(memory_space=pltpu.HBM)
    anywhere = pl.BlockSpec(memory_space=pl.ANY)
    dma = pltpu.SemaphoreType.DMA
    scratch = [
        pltpu.SMEM((2, 1, 1), F32),
        pltpu.VMEM((2, NI, D), BF),
        pltpu.VMEM((2 * NI, D), BF),
        pltpu.VMEM((D, D), BF),
        pltpu.VMEM((NI,), jnp.int32),
        pltpu.VMEM((NI,), jnp.int32),
        pltpu.VMEM((16, 2, D), BF),
        pltpu.VMEM((4, 4, 4, 8, D), BF),
        pltpu.VMEM((512, D), BF),
        pltpu.VMEM((512, 2 * NI), BF),
        pltpu.VMEM((2, D), F32),
        pltpu.VMEM((NI, D), BF),
        pltpu.VMEM((NI, D), BF),
        pltpu.VMEM((NI, D), F32),
        pltpu.VMEM((4, 32, D), F32),
        pltpu.VMEM((4, 4, 32, D), BF),
        pltpu.VMEM((4, 4, 32, D), BF),
        pltpu.VMEM((4, 8, D), F32),
        pltpu.VMEM((4, 4, 8, D), BF),
        pltpu.VMEM((4, 4, 8, D), BF),
        pltpu.VMEM((2, D), F32),
        pltpu.VMEM((16, 2, D), BF),
        pltpu.VMEM((16, 2, D), BF),
        dma((7,)), dma((3,)), dma((3,)), dma((16,)), dma((16,)),
        dma((4, 4)), dma((4, 4)), dma((4, 4)), dma((4, 4)),
        dma((4, 4)), dma((4, 4)), dma((4, 4)), dma((4, 4)), dma((16,)), dma((16,)),
    ]
    return pl.pallas_call(
        kernel,
        out_shape=(
            jax.ShapeDtypeStruct((NI, D), BF),
            jax.ShapeDtypeStruct((2, D), F32),
        ),
        in_specs=[hbm] * 6,
        out_specs=(anywhere, vmem),
        scratch_shapes=scratch,
        compiler_params=pltpu.CompilerParams(
            collective_id=0, has_side_effects=True, vmem_limit_bytes=40 * 2**20
        ),
        cost_estimate=pl.CostEstimate(flops=4 * 10**9, bytes_accessed=8 * 10**6, transcendentals=10**6),
        name="reward_backward",
    )(
        *[pltpu.with_memory_space_constraint(a, pltpu.HBM) for a in (images, texts, text_proj, labels)],
        logit_scale.reshape(1, 1),
        logit_bias.reshape(1, 1),
    )


def solution(mesh):
    in_specs = (P(("blk", "grp"), None), P(("blk", "grp"), None), P(), P(("blk", "grp")), P(), P())
    out_specs = (P(("blk", "grp"), None), P(("blk", "grp"), None))
    return jax.shard_map(local, mesh=mesh, in_specs=in_specs, out_specs=out_specs, check_vma=False)
```

```python
import jax
import jax.numpy as jnp
from jax import lax
from jax.experimental import pallas as pl
from jax.experimental.pallas import tpu as pltpu
from jax.sharding import PartitionSpec as P

MESH = pl.DeviceIdType.MESH
BF = jnp.bfloat16
F32 = jnp.float32
D = 1152
NI = 256
EPS = 1e-06
NT = (((1,), (1,)), ((), ()))
TN = (((0,), (0,)), ((), ()))
STEPS = (0, -1, -2, -3, 1, 2, 3, 4, 5, 6, 7, 8, -4, -5, -6, -7)
NEAR = (7, 6, 3, 5, 2, 4, 1)
SEG = 128
COLS = (slice(0, 640), slice(640, D))
WIDE = (640, 512)
ROWS = {0: 0, 1: SEG, 3: 2 * SEG, 2: 3 * SEG, 4: 4 * SEG}
LESS, MORE = 3 * SEG, 5 * SEG


def mod(a, n):
    return lax.rem(a + n, n)


def unit(v):
    r = lax.rsqrt(jnp.sum(v * v, axis=-1, keepdims=True) + EPS)
    return v * r, r


def kernel(
    images, texts, proj_w, labels, scale_ref, bias_ref,
    out_img, out_txt,
    scal, imgs, emb, wv, wvt, lab_a, lab_b, zin, txa, txb, e_txt, wt, proj_own, gimg_out, gimg_in, gimg,
    own1a, own1b, s1a, s1b, r1a, r1b, own2a, own2b, s2a, s2b, r2a, r2b, own3, zout, zr,
    sem_l, sem_cs, sem_cr, sem_zs, sem_zr, sem_os, sem_or, sem_ss, sem_sr, sem_bs, sem_br,
    sem_1s, sem_1r, sem_2s, sem_2r, sem_3s, sem_3r,
):
    blk = lax.axis_index("blk")
    grp = lax.axis_index("grp")
    c = lax.rem(blk, 2)
    z = lax.rem(grp, 4) * 4 + lax.div(blk, 2)
    x = lax.div(grp, 16)
    y = lax.rem(lax.div(grp, 4), 4)
    wide = pl.when(c == 1)
    narrow = pl.when(c == 0)
    tx, own1, s1, r1 = (txa, txb), (own1a, own1b), (s1a, s1b), (r1a, r1b)
    own2, s2, r2 = (own2a, own2b), (s2a, s2b), (r2a, r2b)
    parts = (0, 1)

    def device(core, dx=0, dy=0, dz=0):
        tz = mod(z + dz, 16)
        return {
            "blk": lax.rem(tz, 4) * 2 + core,
            "grp": mod(x + dx, 4) * 16 + mod(y + dy, 4) * 4 + lax.div(tz, 4),
        }

    def remote(src, dst, ss, rs, core, **to):
        return pltpu.make_async_remote_copy(
            src_ref=src, dst_ref=dst, send_sem=ss, recv_sem=rs,
            device_id=device(core, **to), device_id_type=MESH,
        )

    def along(p, by, first):
        return {"dx" if (p == 0) == first else "dy": by}

    def z_copy(k):
        return remote(zin.at[0], zin.at[k], sem_zs.at[k], sem_zr.at[k], c, dz=STEPS[k])

    def on_copy(s, p):
        to = 3 if s == 0 else 4 - 2 * c
        return remote(
            tx[p].at[s, 0, 0], tx[p].at[to, 0, 0], sem_os.at[s, p], sem_or.at[to, p], c if s == 0 else 1, dz=(-4, 4)[s]
        )

    def on_arrival(s, p):
        return remote(tx[p].at[0, 0, 0], tx[p].at[s, 0, 0], sem_os.at[0, p], sem_or.at[s, p], c, dz=4)

    def small_copy(s, p, d):
        t = tx[p]
        return remote(t.at[s, 0, 0], t.at[s, 0, d], sem_ss.at[s, p, d], sem_sr.at[s, p, d], c, **along(p, d, True))

    def bulk_copy(s, p, d):
        t = tx[p]
        return remote(t.at[s, 0], t.at[s, d], sem_bs.at[s, p, d], sem_br.at[s, p, d], c, **along(p, d, False))

    def first_copy(s, p, d):
        return remote(s1[p].at[s, d], r1[p].at[s, d], sem_1s.at[s, p, d], sem_1r.at[s, p, d], c, **along(p, -d, False))

    def second_copy(s, p, d):
        return remote(s2[p].at[s, d], r2[p].at[s, d], sem_2s.at[s, p, d], sem_2r.at[s, p, d], c, **along(p, -d, True))

    def third_copy(k):
        return remote(zout.at[k], zr.at[k], sem_3s.at[k], sem_3r.at[k], c, dz=-STEPS[k])

    def third_extra(k):
        return remote(zout.at[k + 8], zr.at[k], sem_3s.at[k + 8], sem_3r.at[k], 0, dz=-STEPS[k])

    fan = [(d, p) for d in (2, 1, 3) for p in parts]

    load_txt = pltpu.make_async_copy(texts, zin.at[0], sem_l.at[0])
    load_lab = pltpu.make_async_copy(labels, lab_a, sem_l.at[1])
    load_img = pltpu.make_async_copy(images, imgs.at[0], sem_l.at[2])
    rest = [
        pltpu.make_async_copy(proj_w, wv, sem_l.at[3]),
        pltpu.make_async_copy(scale_ref, scal.at[0], sem_l.at[5]),
        pltpu.make_async_copy(bias_ref, scal.at[1], sem_l.at[6]),
    ]
    for cp in [load_txt, load_lab, load_img] + rest:
        cp.start()

    barrier = pltpu.get_barrier_semaphore()
    chips = [dict(dz=d) for d in (4, -4, 3, -3, 2, -2, 1, -1)]
    chips += [dict(dx=d) for d in (1, 2, 3)] + [dict(dy=d) for d in (1, 2, 3)]
    for p in chips:
        pl.semaphore_signal(barrier, inc=1, device_id=device(c, **p), device_id_type=MESH)
    pl.semaphore_signal(barrier, inc=1, device_id=device(1 - c), device_id_type=MESH)

    @wide
    def _():
        pl.semaphore_signal(barrier, inc=1, device_id=device(0, dz=-4), device_id_type=MESH)

    load_txt.wait()

    @narrow
    def _():
        pl.semaphore_wait(barrier, len(chips) + 2)

    @wide
    def _():
        pl.semaphore_wait(barrier, len(chips) + 1)

    for k in NEAR:
        z_copy(k).start()

    load_lab.wait()
    load_img.wait()
    core_lab = remote(lab_a, lab_b, sem_cs.at[0], sem_cr.at[0], 1 - c)
    core_img = remote(imgs.at[0], imgs.at[1], sem_cs.at[1], sem_cr.at[1], 1 - c)
    core_lab.start()
    core_img.start()

    def embed(half):
        def step(i, carry):
            u, _ = unit(imgs[half, pl.ds(pl.multiple_of(i * 64, 64), 64), :].astype(F32))
            emb[pl.ds(pl.multiple_of(half * NI + i * 64, 64), 64), :] = u.astype(BF)
            return carry
        lax.fori_loop(0, NI // 64, step, 0)

    embed(0)

    def place(s):
        for k in range(4 * s, 4 * s + 4):
            if k:
                z_copy(k).wait_recv()
        rows = zin[4 * s : 4 * s + 4].astype(F32).reshape(8, D).astype(BF)
        for p in parts:
            tx[p][s, 0, 0] = rows[:, COLS[p]]
            on_copy(s, p).start()

    def small(s):
        for d, p in fan:
            small_copy(s, p, d).start()

    def arrive(s):
        for p in parts:
            on_arrival(s, p).wait_recv()
        small(s)

    def spread(s):
        for d, p in fan:
            small_copy(s, p, d).wait_recv()
        for d, p in fan:
            bulk_copy(s, p, d).start()

    for s in (0, 1):
        place(s)
        small(s)
    spread(0)
    spread(1)
    core_lab.wait()
    core_img.wait()
    embed(1)
    for cp in rest:
        cp.wait()
    proj_own[...] = jnp.dot(zin[0], wv[...], preferred_element_type=F32)
    wvt[...] = wv[...].T
    arrive(3)

    @wide
    def _():
        arrive(2)
        arrive(4)

    spread(3)

    @wide
    def _():
        spread(2)
        spread(4)

    scale = scal[0, 0, 0]
    bias = scal[1, 0, 0]

    lab = jnp.concatenate([lab_a[...][None, :], lab_b[...][None, :]], axis=1)
    ez = mod(z - (((lab >> 1) & 3) * 4 + ((lab >> 8) & 3)), 16)
    ey = mod(y - ((lab >> 3) & 3), 4)
    ex = mod(x - ((lab >> 5) & 3), 4)
    kz = jnp.where(ez == 0, 0, jnp.where(ez <= 8, ez + 3, jnp.where(ez >= 13, 16 - ez, 24 - ez)))
    seg = kz >> 2
    base = jnp.where(seg == 3, ROWS[3], jnp.where(seg == 2, ROWS[2], seg * SEG))
    within = ey * 32 + ex * 8 + (kz & 3) * 2 + (lab & 1)
    owner = (lab >> 7) & 1
    pos = jnp.where((seg == 2) & (c == 0), -1, base + within)
    pos = jnp.where(owner == c, pos, jnp.where((seg == 2) & (c == 1), ROWS[4] + within, -1))

    def segment(s):
        for d, p in fan:
            bulk_copy(s, p, d).wait_recv()
        rows = pl.ds(ROWS[s], SEG)
        ta = txa[s].reshape(SEG, WIDE[0])
        tb = jnp.concatenate([txb[s, j, i] for i in range(4) for j in range(4)], axis=0)
        p = jnp.dot(ta, wv[COLS[0], :], preferred_element_type=F32)
        p = p + jnp.dot(tb, wv[COLS[1], :], preferred_element_type=F32)
        e = unit(p)[0].astype(BF)
        e_txt[rows, :] = e
        logits = scale * lax.dot_general(e, emb[...], NT, preferred_element_type=F32) + bias
        match = lax.broadcasted_iota(jnp.int32, logits.shape, 0) + ROWS[s] == pos
        sg = scale / (1.0 + jnp.exp(jnp.where(match, logits, -logits)))
        w = jnp.where(match, -sg, sg).astype(BF)
        wt[rows, :] = w
        g = jnp.dot(w, emb[...], preferred_element_type=F32)
        own1a[s] = g[:32, COLS[0]]
        s1a[s] = g[:, COLS[0]].astype(BF).reshape(4, 32, WIDE[0])
        for i in range(4):
            for j in range(4):
                b = g[i * 32 + j * 8 : i * 32 + j * 8 + 8, COLS[1]]
                if j == 0:
                    own1b[s, i] = b
                else:
                    s1b[s, j, i] = b.astype(BF)
        for d, p in fan:
            first_copy(s, p, d).start()

    for s in (0, 1, 3):
        segment(s)

    @wide
    def _():
        segment(2)
        segment(4)

    def image_part(half):
        def over(n):
            def step(i, carry):
                cols = pl.ds(pl.multiple_of(half * NI + i * 128, 128), 128)
                g = lax.dot_general(wt[:n, cols], e_txt[:n, :], TN, preferred_element_type=F32)
                rows = pl.ds(pl.multiple_of(i * 128, 128), 128)
                if half == 1:
                    gimg_out[rows, :] = g.astype(BF)
                else:
                    gimg[rows, :] = g
                return carry
            lax.fori_loop(0, 2, step, 0)

        @narrow
        def _():
            over(LESS)

        @wide
        def _():
            over(MORE)

    image_part(1)
    core_grad = remote(gimg_out, gimg_in, sem_cs.at[2], sem_cr.at[2], 1 - c)
    core_grad.start()

    def second(s):
        for p in parts:
            shape = (4, 8, WIDE[p])
            acc = own1[p][s].reshape(shape)
            for d in (1, 2, 3):
                first_copy(s, p, d).wait_recv()
                acc = acc + r1[p][s, d].astype(F32).reshape(shape)
            own2[p][s] = acc[0]
            s2[p][s] = acc.astype(BF)
            for d in (2, 1, 3):
                second_copy(s, p, d).start()

    def third(s):
        sums = []
        for p in parts:
            acc = own2[p][s]
            for d in (1, 2, 3):
                second_copy(s, p, d).wait_recv()
                acc = acc + r2[p][s, d].astype(F32)
            sums.append(acc)
        acc = jnp.concatenate(sums, axis=1)
        for i in (3, 2, 1, 0):
            row = acc[2 * i : 2 * i + 2, :]
            if s == 4:
                zout[16 + i] = row.astype(BF)
                third_extra(8 + i).start()
            elif s == i == 0:
                own3[...] = row
            else:
                zout[4 * s + i] = row.astype(BF)
                third_copy(4 * s + i).start()

    second(0)
    second(1)
    image_part(0)
    second(3)

    @wide
    def _():
        second(2)
        second(4)

    third(0)
    third(1)
    third(3)

    @wide
    def _():
        third(2)
        third(4)

    core_grad.wait()

    def finish(i, carry):
        rows = pl.ds(pl.multiple_of(i * 64, 64), 64)
        g = gimg[rows, :] + gimg_in[rows, :].astype(F32)
        u, r = unit(imgs[0, rows, :].astype(F32))
        g = (g - u * jnp.sum(u * g, axis=-1, keepdims=True)) * r
        gimg_out[rows, :] = g.astype(BF)
        return carry

    lax.fori_loop(0, NI // 64, finish, 0)
    store = pltpu.make_async_copy(gimg_out, out_img, sem_l.at[4])
    store.start()

    def left(s):
        for d, p in fan:
            small_copy(s, p, d).wait_send()
            bulk_copy(s, p, d).wait_send()
            first_copy(s, p, d).wait_send()
            second_copy(s, p, d).wait_send()

    for k in NEAR:
        z_copy(k).wait_send()
    for s in (0, 1):
        for p in parts:
            on_copy(s, p).wait_send()
    for s in (0, 1, 3):
        left(s)
    for k in (1, 2, 3, 4, 5, 6, 7, 12, 13, 14, 15):
        third_copy(k).wait_send()

    @wide
    def _():
        left(2)
        left(4)
        for k in (8, 9, 10, 11):
            third_copy(k).wait_send()
            third_extra(k).wait_send()

    store.wait()
    u, r = unit(proj_own[...])
    for k in range(1, 16):
        third_copy(k).wait_recv()
    total = own3[...]
    for k in range(1, 16):
        total = total + zr[k].astype(F32)
    pg = ((total - u * jnp.sum(u * total, axis=-1, keepdims=True)) * r).astype(BF)
    out_txt[...] = jnp.dot(pg, wvt[...], preferred_element_type=F32)


def local(images, texts, text_proj, labels, logit_scale, logit_bias):
    vmem = pl.BlockSpec(memory_space=pltpu.VMEM)
    hbm = pl.BlockSpec(memory_space=pltpu.HBM)
    anywhere = pl.BlockSpec(memory_space=pl.ANY)
    dma = pltpu.SemaphoreType.DMA
    scratch = [
        pltpu.SMEM((2, 1, 1), F32),
        pltpu.VMEM((2, NI, D), BF),
        pltpu.VMEM((2 * NI, D), BF),
        pltpu.VMEM((D, D), BF),
        pltpu.VMEM((D, D), BF),
        pltpu.VMEM((NI,), jnp.int32),
        pltpu.VMEM((NI,), jnp.int32),
        pltpu.VMEM((8, 2, D), BF),
        *[pltpu.VMEM((5, 4, 4, 8, w), BF) for w in WIDE],
        pltpu.VMEM((MORE, D), BF),
        pltpu.VMEM((MORE, 2 * NI), BF),
        pltpu.VMEM((2, D), F32),
        pltpu.VMEM((NI, D), BF),
        pltpu.VMEM((NI, D), BF),
        pltpu.VMEM((NI, D), F32),
        pltpu.VMEM((5, 32, WIDE[0]), F32),
        pltpu.VMEM((5, 4, 8, WIDE[1]), F32),
        pltpu.VMEM((5, 4, 32, WIDE[0]), BF),
        pltpu.VMEM((5, 4, 4, 8, WIDE[1]), BF),
        pltpu.VMEM((5, 4, 32, WIDE[0]), BF),
        pltpu.VMEM((5, 4, 4, 8, WIDE[1]), BF),
        *[pltpu.VMEM((5, 8, w), F32) for w in WIDE],
        *[pltpu.VMEM((5, 4, 8, w), BF) for w in WIDE],
        *[pltpu.VMEM((5, 4, 8, w), BF) for w in WIDE],
        pltpu.VMEM((2, D), F32),
        pltpu.VMEM((20, 2, D), BF),
        pltpu.VMEM((16, 2, D), BF),
        dma((7,)), dma((3,)), dma((3,)),
        dma((8,)), dma((8,)), dma((2, 2)), dma((5, 2)),
        *[dma((5, 2, 4)) for _ in range(8)], dma((20,)), dma((16,)),
    ]
    return pl.pallas_call(
        kernel,
        out_shape=(
            jax.ShapeDtypeStruct((NI, D), BF),
            jax.ShapeDtypeStruct((2, D), F32),
        ),
        in_specs=[hbm] * 6,
        out_specs=(anywhere, vmem),
        scratch_shapes=scratch,
        compiler_params=pltpu.CompilerParams(
            collective_id=0, has_side_effects=True, vmem_limit_bytes=40 * 2**20
        ),
        cost_estimate=pl.CostEstimate(flops=4 * 10**9, bytes_accessed=8 * 10**6, transcendentals=10**6),
        name="reward_backward",
    )(
        *[pltpu.with_memory_space_constraint(a, pltpu.HBM) for a in (images, texts, text_proj, labels)],
        logit_scale.reshape(1, 1),
        logit_bias.reshape(1, 1),
    )


def solution(mesh):
    in_specs = (P(("blk", "grp"), None), P(("blk", "grp"), None), P(), P(("blk", "grp")), P(), P())
    out_specs = (P(("blk", "grp"), None), P(("blk", "grp"), None))
    return jax.shard_map(local, mesh=mesh, in_specs=in_specs, out_specs=out_specs, check_vma=False)
```

```python
import jax
import jax.numpy as jnp
from jax import lax
from jax.experimental import pallas as pl
from jax.experimental.pallas import tpu as pltpu
from jax.sharding import PartitionSpec as P

MESH = pl.DeviceIdType.MESH
BF = jnp.bfloat16
F32 = jnp.float32
D = 1152
NI = 256
EPS = 1e-06
NT = (((1,), (1,)), ((), ()))
TN = (((0,), (0,)), ((), ()))
STEPS = (0, -1, -2, -3, 1, 2, 3, 4, 5, 6, 7, 8, -4, -5, -6, -7)
NEAR = (7, 6, 3, 5, 2, 4, 1)
SEG = 128
COLS = (slice(0, 640), slice(640, D))
WIDE = (640, 512)
ROWS = {0: 0, 1: SEG, 3: 2 * SEG, 2: 3 * SEG, 4: 4 * SEG}
LESS, MORE = 3 * SEG, 5 * SEG


def mod(a, n):
    return lax.rem(a + n, n)


def unit(v):
    r = lax.rsqrt(jnp.sum(v * v, axis=-1, keepdims=True) + EPS)
    return v * r, r


def kernel(
    images, texts, proj_w, labels, scale_ref, bias_ref,
    out_img, out_txt,
    scal, imgs, emb, wv, wvt, lab_a, lab_b, zin, txa, txb, e_txt, wt, proj_own, gimg_out, gimg_in, gimg,
    own1a, own1b, s1a, s1b, r1a, r1b, own2a, own2b, s2a, s2b, r2a, r2b, own3, zout, zr,
    sem_l, sem_cs, sem_cr, sem_zs, sem_zr, sem_os, sem_or, sem_ss, sem_sr, sem_bs, sem_br,
    sem_1s, sem_1r, sem_2s, sem_2r, sem_3s, sem_3r,
):
    blk = lax.axis_index("blk")
    grp = lax.axis_index("grp")
    c = lax.rem(blk, 2)
    z = lax.rem(grp, 4) * 4 + lax.div(blk, 2)
    x = lax.div(grp, 16)
    y = lax.rem(lax.div(grp, 4), 4)
    wide = pl.when(c == 1)
    narrow = pl.when(c == 0)
    tx, own1, s1, r1 = (txa, txb), (own1a, own1b), (s1a, s1b), (r1a, r1b)
    own2, s2, r2 = (own2a, own2b), (s2a, s2b), (r2a, r2b)
    parts = (0, 1)

    def device(core, dx=0, dy=0, dz=0):
        tz = mod(z + dz, 16)
        return {
            "blk": lax.rem(tz, 4) * 2 + core,
            "grp": mod(x + dx, 4) * 16 + mod(y + dy, 4) * 4 + lax.div(tz, 4),
        }

    def remote(src, dst, ss, rs, core, **to):
        return pltpu.make_async_remote_copy(
            src_ref=src, dst_ref=dst, send_sem=ss, recv_sem=rs,
            device_id=device(core, **to), device_id_type=MESH,
        )

    def along(p, by, first):
        return {"dx" if (p == 0) == first else "dy": by}

    def z_copy(k):
        return remote(zin.at[0], zin.at[k], sem_zs.at[k], sem_zr.at[k], c, dz=STEPS[k])

    def on_copy(s, p):
        to = 3 if s == 0 else 4 - 2 * c
        return remote(
            tx[p].at[s, 0, 0], tx[p].at[to, 0, 0], sem_os.at[s, p], sem_or.at[to, p], c if s == 0 else 1, dz=(-4, 4)[s]
        )

    def on_arrival(s, p):
        return remote(tx[p].at[0, 0, 0], tx[p].at[s, 0, 0], sem_os.at[0, p], sem_or.at[s, p], c, dz=4)

    def small_copy(s, p, d):
        t = tx[p]
        return remote(t.at[s, 0, 0], t.at[s, 0, d], sem_ss.at[s, p, d], sem_sr.at[s, p, d], c, **along(p, d, True))

    def bulk_copy(s, p, d):
        t = tx[p]
        return remote(t.at[s, 0], t.at[s, d], sem_bs.at[s, p, d], sem_br.at[s, p, d], c, **along(p, d, False))

    def first_copy(s, p, d):
        return remote(s1[p].at[s, d], r1[p].at[s, d], sem_1s.at[s, p, d], sem_1r.at[s, p, d], c, **along(p, -d, False))

    def second_copy(s, p, d):
        return remote(s2[p].at[s, d], r2[p].at[s, d], sem_2s.at[s, p, d], sem_2r.at[s, p, d], c, **along(p, -d, True))

    def third_copy(k):
        return remote(zout.at[k], zr.at[k], sem_3s.at[k], sem_3r.at[k], c, dz=-STEPS[k])

    def third_extra(k):
        return remote(zout.at[k + 8], zr.at[k], sem_3s.at[k + 8], sem_3r.at[k], 0, dz=-STEPS[k])

    fan = [(d, p) for d in (2, 1, 3) for p in parts]

    load_txt = pltpu.make_async_copy(texts, zin.at[0], sem_l.at[0])
    load_lab = pltpu.make_async_copy(labels, lab_a, sem_l.at[1])
    load_img = pltpu.make_async_copy(images, imgs.at[0], sem_l.at[2])
    rest = [
        pltpu.make_async_copy(proj_w, wv, sem_l.at[3]),
        pltpu.make_async_copy(scale_ref, scal.at[0], sem_l.at[5]),
        pltpu.make_async_copy(bias_ref, scal.at[1], sem_l.at[6]),
    ]
    for cp in [load_txt, load_lab, load_img] + rest:
        cp.start()

    barrier = pltpu.get_barrier_semaphore()
    chips = [dict(dz=d) for d in (4, -4, 3, -3, 2, -2, 1, -1)]
    chips += [dict(dx=d) for d in (1, 2, 3)] + [dict(dy=d) for d in (1, 2, 3)]
    for p in chips:
        pl.semaphore_signal(barrier, inc=1, device_id=device(c, **p), device_id_type=MESH)
    pl.semaphore_signal(barrier, inc=1, device_id=device(1 - c), device_id_type=MESH)

    @wide
    def _():
        pl.semaphore_signal(barrier, inc=1, device_id=device(0, dz=-4), device_id_type=MESH)

    load_txt.wait()

    @narrow
    def _():
        pl.semaphore_wait(barrier, len(chips) + 2)

    @wide
    def _():
        pl.semaphore_wait(barrier, len(chips) + 1)

    for k in NEAR:
        z_copy(k).start()

    load_lab.wait()
    load_img.wait()
    core_lab = remote(lab_a, lab_b, sem_cs.at[0], sem_cr.at[0], 1 - c)
    core_img = remote(imgs.at[0], imgs.at[1], sem_cs.at[1], sem_cr.at[1], 1 - c)
    core_lab.start()
    core_img.start()

    def embed(half):
        def step(i, carry):
            u, _ = unit(imgs[half, pl.ds(pl.multiple_of(i * 64, 64), 64), :].astype(F32))
            emb[pl.ds(pl.multiple_of(half * NI + i * 64, 64), 64), :] = u.astype(BF)
            return carry
        lax.fori_loop(0, NI // 64, step, 0)

    embed(0)

    def place(s):
        for k in range(4 * s, 4 * s + 4):
            if k:
                z_copy(k).wait_recv()
        rows = zin[4 * s : 4 * s + 4].astype(F32).reshape(8, D).astype(BF)
        for p in parts:
            tx[p][s, 0, 0] = rows[:, COLS[p]]
            on_copy(s, p).start()

    def small(s):
        for d, p in fan:
            small_copy(s, p, d).start()

    def arrive(s):
        for p in parts:
            on_arrival(s, p).wait_recv()
        small(s)

    def spread(s):
        for d, p in fan:
            small_copy(s, p, d).wait_recv()
        for d, p in fan:
            bulk_copy(s, p, d).start()

    for s in (0, 1):
        place(s)
        small(s)
    spread(0)
    spread(1)
    core_lab.wait()
    core_img.wait()
    embed(1)
    arrive(3)

    @wide
    def _():
        arrive(2)
        arrive(4)

    for cp in rest:
        cp.wait()
    proj_own[...] = jnp.dot(zin[0], wv[...], preferred_element_type=F32)
    wvt[...] = wv[...].T
    spread(3)

    @wide
    def _():
        spread(2)
        spread(4)

    scale = scal[0, 0, 0]
    bias = scal[1, 0, 0]

    lab = jnp.concatenate([lab_a[...][None, :], lab_b[...][None, :]], axis=1)
    ez = mod(z - (((lab >> 1) & 3) * 4 + ((lab >> 8) & 3)), 16)
    ey = mod(y - ((lab >> 3) & 3), 4)
    ex = mod(x - ((lab >> 5) & 3), 4)
    kz = jnp.where(ez == 0, 0, jnp.where(ez <= 8, ez + 3, jnp.where(ez >= 13, 16 - ez, 24 - ez)))
    seg = kz >> 2
    base = jnp.where(seg == 3, ROWS[3], jnp.where(seg == 2, ROWS[2], seg * SEG))
    within = ey * 32 + ex * 8 + (kz & 3) * 2 + (lab & 1)
    owner = (lab >> 7) & 1
    pos = jnp.where((seg == 2) & (c == 0), -1, base + within)
    pos = jnp.where(owner == c, pos, jnp.where((seg == 2) & (c == 1), ROWS[4] + within, -1))

    def segment(s):
        for d, p in fan:
            bulk_copy(s, p, d).wait_recv()
        rows = pl.ds(ROWS[s], SEG)
        ta = txa[s].reshape(SEG, WIDE[0])
        tb = jnp.concatenate([txb[s, j, i] for i in range(4) for j in range(4)], axis=0)
        p = jnp.dot(ta, wv[COLS[0], :], preferred_element_type=F32)
        p = p + jnp.dot(tb, wv[COLS[1], :], preferred_element_type=F32)
        e = unit(p)[0].astype(BF)
        e_txt[rows, :] = e
        logits = scale * lax.dot_general(e, emb[...], NT, preferred_element_type=F32) + bias
        match = lax.broadcasted_iota(jnp.int32, logits.shape, 0) + ROWS[s] == pos
        sg = scale / (1.0 + jnp.exp(jnp.where(match, logits, -logits)))
        w = jnp.where(match, -sg, sg).astype(BF)
        wt[rows, :] = w
        g = jnp.dot(w, emb[...], preferred_element_type=F32)
        own1a[s] = g[:32, COLS[0]]
        s1a[s] = g[:, COLS[0]].astype(BF).reshape(4, 32, WIDE[0])
        for i in range(4):
            for j in range(4):
                b = g[i * 32 + j * 8 : i * 32 + j * 8 + 8, COLS[1]]
                if j == 0:
                    own1b[s, i] = b
                else:
                    s1b[s, j, i] = b.astype(BF)
        for d, p in fan:
            first_copy(s, p, d).start()

    for s in (0, 1, 3):
        segment(s)

    @wide
    def _():
        segment(2)
        segment(4)

    def image_part(half):
        def over(n):
            def step(i, carry):
                cols = pl.ds(pl.multiple_of(half * NI + i * 128, 128), 128)
                g = lax.dot_general(wt[:n, cols], e_txt[:n, :], TN, preferred_element_type=F32)
                rows = pl.ds(pl.multiple_of(i * 128, 128), 128)
                if half == 1:
                    gimg_out[rows, :] = g.astype(BF)
                else:
                    gimg[rows, :] = g
                return carry
            lax.fori_loop(0, 2, step, 0)

        @narrow
        def _():
            over(LESS)

        @wide
        def _():
            over(MORE)

    image_part(1)
    core_grad = remote(gimg_out, gimg_in, sem_cs.at[2], sem_cr.at[2], 1 - c)
    core_grad.start()

    def second(s):
        for p in parts:
            shape = (4, 8, WIDE[p])
            acc = own1[p][s].reshape(shape)
            for d in (1, 2, 3):
                first_copy(s, p, d).wait_recv()
                acc = acc + r1[p][s, d].astype(F32).reshape(shape)
            own2[p][s] = acc[0]
            s2[p][s] = acc.astype(BF)
            for d in (2, 1, 3):
                second_copy(s, p, d).start()

    def third(s):
        sums = []
        for p in parts:
            acc = own2[p][s]
            for d in (1, 2, 3):
                second_copy(s, p, d).wait_recv()
                acc = acc + r2[p][s, d].astype(F32)
            sums.append(acc)
        acc = jnp.concatenate(sums, axis=1)
        for i in (3, 2, 1, 0):
            row = acc[2 * i : 2 * i + 2, :]
            if s == 4:
                zout[16 + i] = row.astype(BF)
                third_extra(8 + i).start()
            elif s == i == 0:
                own3[...] = row
            else:
                zout[4 * s + i] = row.astype(BF)
                third_copy(4 * s + i).start()

    second(0)
    second(1)
    image_part(0)
    second(3)

    @wide
    def _():
        second(2)
        second(4)

    third(0)
    third(1)
    third(3)

    @wide
    def _():
        third(2)
        third(4)

    core_grad.wait()

    def finish(i, carry):
        rows = pl.ds(pl.multiple_of(i * 64, 64), 64)
        g = gimg[rows, :] + gimg_in[rows, :].astype(F32)
        u, r = unit(imgs[0, rows, :].astype(F32))
        g = (g - u * jnp.sum(u * g, axis=-1, keepdims=True)) * r
        gimg_out[rows, :] = g.astype(BF)
        return carry

    lax.fori_loop(0, NI // 64, finish, 0)
    store = pltpu.make_async_copy(gimg_out, out_img, sem_l.at[4])
    store.start()

    def left(s):
        for d, p in fan:
            small_copy(s, p, d).wait_send()
            bulk_copy(s, p, d).wait_send()
            first_copy(s, p, d).wait_send()
            second_copy(s, p, d).wait_send()

    for k in NEAR:
        z_copy(k).wait_send()
    for s in (0, 1):
        for p in parts:
            on_copy(s, p).wait_send()
    for s in (0, 1, 3):
        left(s)
    for k in (1, 2, 3, 4, 5, 6, 7, 12, 13, 14, 15):
        third_copy(k).wait_send()

    @wide
    def _():
        left(2)
        left(4)
        for k in (8, 9, 10, 11):
            third_copy(k).wait_send()
            third_extra(k).wait_send()

    store.wait()
    u, r = unit(proj_own[...])
    total = own3[...]
    for k in range(1, 16):
        third_copy(k).wait_recv()
        total = total + zr[k].astype(F32)
    pg = ((total - u * jnp.sum(u * total, axis=-1, keepdims=True)) * r).astype(BF)
    out_txt[...] = jnp.dot(pg, wvt[...], preferred_element_type=F32)


def local(images, texts, text_proj, labels, logit_scale, logit_bias):
    vmem = pl.BlockSpec(memory_space=pltpu.VMEM)
    hbm = pl.BlockSpec(memory_space=pltpu.HBM)
    anywhere = pl.BlockSpec(memory_space=pl.ANY)
    dma = pltpu.SemaphoreType.DMA
    scratch = [
        pltpu.SMEM((2, 1, 1), F32),
        pltpu.VMEM((2, NI, D), BF),
        pltpu.VMEM((2 * NI, D), BF),
        pltpu.VMEM((D, D), BF),
        pltpu.VMEM((D, D), BF),
        pltpu.VMEM((NI,), jnp.int32),
        pltpu.VMEM((NI,), jnp.int32),
        pltpu.VMEM((8, 2, D), BF),
        *[pltpu.VMEM((5, 4, 4, 8, w), BF) for w in WIDE],
        pltpu.VMEM((MORE, D), BF),
        pltpu.VMEM((MORE, 2 * NI), BF),
        pltpu.VMEM((2, D), F32),
        pltpu.VMEM((NI, D), BF),
        pltpu.VMEM((NI, D), BF),
        pltpu.VMEM((NI, D), F32),
        pltpu.VMEM((5, 32, WIDE[0]), F32),
        pltpu.VMEM((5, 4, 8, WIDE[1]), F32),
        pltpu.VMEM((5, 4, 32, WIDE[0]), BF),
        pltpu.VMEM((5, 4, 4, 8, WIDE[1]), BF),
        pltpu.VMEM((5, 4, 32, WIDE[0]), BF),
        pltpu.VMEM((5, 4, 4, 8, WIDE[1]), BF),
        *[pltpu.VMEM((5, 8, w), F32) for w in WIDE],
        *[pltpu.VMEM((5, 4, 8, w), BF) for w in WIDE],
        *[pltpu.VMEM((5, 4, 8, w), BF) for w in WIDE],
        pltpu.VMEM((2, D), F32),
        pltpu.VMEM((20, 2, D), BF),
        pltpu.VMEM((16, 2, D), BF),
        dma((7,)), dma((3,)), dma((3,)),
        dma((8,)), dma((8,)), dma((2, 2)), dma((5, 2)),
        *[dma((5, 2, 4)) for _ in range(8)], dma((20,)), dma((16,)),
    ]
    return pl.pallas_call(
        kernel,
        out_shape=(
            jax.ShapeDtypeStruct((NI, D), BF),
            jax.ShapeDtypeStruct((2, D), F32),
        ),
        in_specs=[hbm] * 6,
        out_specs=(anywhere, vmem),
        scratch_shapes=scratch,
        compiler_params=pltpu.CompilerParams(
            collective_id=0, has_side_effects=True, vmem_limit_bytes=40 * 2**20
        ),
        cost_estimate=pl.CostEstimate(flops=4 * 10**9, bytes_accessed=8 * 10**6, transcendentals=10**6),
        name="reward_backward",
    )(
        *[pltpu.with_memory_space_constraint(a, pltpu.HBM) for a in (images, texts, text_proj, labels)],
        logit_scale.reshape(1, 1),
        logit_bias.reshape(1, 1),
    )


def solution(mesh):
    in_specs = (P(("blk", "grp"), None), P(("blk", "grp"), None), P(), P(("blk", "grp")), P(), P())
    out_specs = (P(("blk", "grp"), None), P(("blk", "grp"), None))
    return jax.shard_map(local, mesh=mesh, in_specs=in_specs, out_specs=out_specs, check_vma=False)
```
